128 devices in a mesh: layer: 4 (over x), trace: 32 (over z, y, core).
Axes of the slice: x: 4, y: 4, z: 4, core: 2. Of those that a mesh axis runs over, the one named last changes fastest.
Arguments:
- operators: bfloat16 [4, 768, 512, 512], P('layer', 'trace'), may hold values from -0.15625 to 0.15625
- sources: bfloat16 [4, 2, 131072, 128], P('layer', None, 'trace'), may hold values from -6 to 6
- row_block: int32 [4, 32, 24], P('layer'), may hold values from 0 to 255, as said below
- col_block: int32 [4, 32, 24], P('layer', 'trace'), may hold values from 0 to 255, as said below
Outputs:
- traces: bfloat16 [4, 2, 131072, 128], P('layer', None, 'trace')
The draws below stay inside these ranges and needn't reach their ends.
Inputs may be any that keep to these rules, and one draw needn't show every extreme that they name: `row_block`: for each layer and each trace index d, the 24 row blocks name distinct owners; in each layer some owner is named by every d, and so are owners 0 and 31. `col_block`: entries of trace index d lie in d * 8 to (d + 1) * 8 - 1.
All inputs are finite; a program needn't handle non-finite values.
Results may differ from the reference program's by a relative error of at most 0.0077.
Values may be sent and summed in bfloat16 or wider, within the bound.
A program may use at most 128 MiB of HBM per device.

```python
import jax
import jax.numpy as jnp
from jax import lax

TRACE_ROWS = 131072
BLOCK = 512
SHOTS = 128
BATCHES = 2
N_LAYERS = 4
BLK_DEV = 8
BLOCKS_DEV = 24
N_LAYER = 4
N_TRACE = 32


def pattern(key):
    base = jax.random.fold_in(key, 7)
    hotter = jax.random.randint(jax.random.fold_in(base, 1), (N_LAYER,), 0, N_TRACE)
    keys = jax.random.split(jax.random.fold_in(base, 2), N_LAYER * N_TRACE)
    orders = jax.vmap(lambda sub: jax.random.permutation(sub, N_TRACE))(keys).reshape(N_LAYER, N_TRACE, N_TRACE)
    place = jnp.arange(N_TRACE)
    forced = (orders == hotter[:, None, None]) | (orders == 0) | (orders == N_TRACE - 1)
    score = jnp.where(forced, -1, place[None, None, :])
    picked = jnp.argsort(score, axis=-1, stable=True)[..., :BLOCKS_DEV]
    owners = jnp.take_along_axis(orders, picked, axis=-1)
    local = jax.random.randint(jax.random.fold_in(base, 3), (N_LAYER, N_TRACE, BLOCKS_DEV), 0, BLK_DEV)
    sender = jnp.arange(N_TRACE)[None, :, None]
    local = jnp.where((sender == 0) & (owners == N_TRACE - 1), BLK_DEV - 1, local)
    local = jnp.where((sender == 0) & (owners == 0), 0, local)
    rows = owners * BLK_DEV + local
    col_local = jax.random.randint(jax.random.fold_in(base, 4), (N_LAYER, N_TRACE, BLOCKS_DEV), 0, BLK_DEV)
    which = jnp.arange(BLOCKS_DEV)[None, None, :]
    col_local = jnp.where((sender == 0) & (which == 0), 0, col_local)
    col_local = jnp.where((sender == N_TRACE - 1) & (which == 0), BLK_DEV - 1, col_local)
    cols = sender * BLK_DEV + col_local
    return (rows.astype(jnp.int32), cols.astype(jnp.int32))


def draw_row_block(key, part):
    return pattern(key)[0]


def draw_col_block(key, part):
    return pattern(key)[1]


def block_scale(own_key, dims, shards, least, largest):
    def one(position, parts):
        heights = jax.random.uniform(jax.random.fold_in(jax.random.fold_in(own_key, 6), position), (parts,), jnp.float32, least / len(shards), largest / len(shards))
        return jnp.repeat(jnp.exp(heights), dims[position] // parts).reshape((-1,) + (1,) * (len(dims) - position - 1))

    level = one(*shards[0])
    for cut in shards[1:]:
        level = level * one(*cut)
    return level


def gaussian(own_key, dims, scale, bound, cuts=(), held_as=jnp.bfloat16):
    loudness = block_scale(own_key, dims, cuts, -0.22, 0.18) if cuts else 1.0
    entries = jax.random.normal(own_key, dims, jnp.float32) * scale * loudness
    return jnp.minimum(jnp.maximum(entries, -bound), bound).astype(held_as)


def setup_inputs(seed: int = 0) -> dict:
    key_list = jax.random.split(jax.random.key(seed), 5)
    return {
        "operators": gaussian(key_list[0], (N_LAYERS, N_TRACE * BLOCKS_DEV, BLOCK, BLOCK), (BLOCK * max(1, BLOCKS_DEV * N_TRACE // (TRACE_ROWS // BLOCK))) ** -0.5, 0.15625, ((0, 4), (1, 32))),
        "sources": gaussian(key_list[1], (N_LAYERS, BATCHES, TRACE_ROWS, SHOTS), 1.0, 6.0, ((0, 4), (2, 32))),
        "row_block": draw_row_block(jax.random.fold_in(key_list[4], 71), 0),
        "col_block": draw_col_block(jax.random.fold_in(key_list[4], 71), 0),
    }


def reference(operators, sources, row_block, col_block):
    count = TRACE_ROWS // BLOCK
    incoming = jnp.zeros((BATCHES, TRACE_ROWS, SHOTS), jnp.bfloat16)
    layers_out = []
    for layer in range(N_LAYERS):
        blocks = operators[layer].reshape(N_TRACE, BLOCKS_DEV, BLOCK, BLOCK)
        rows = row_block[layer].reshape(-1)
        cols = col_block[layer]
        outgoing = []
        for batch in range(BATCHES):
            field = (incoming[batch].astype(jnp.float32) + sources[layer, batch].astype(jnp.float32)).astype(jnp.bfloat16)
            tiles = field.reshape(count, BLOCK, SHOTS)

            def one_device(pair):
                mats, picks = pair
                pieces = tiles[picks]
                prod = jnp.einsum("kij,kjs->kis", mats.astype(jnp.float32), pieces.astype(jnp.float32))
                return prod.astype(jnp.bfloat16)

            prods = lax.map(one_device, (blocks, cols))
            summed = jax.ops.segment_sum(prods.reshape(-1, BLOCK, SHOTS).astype(jnp.float32), rows, num_segments=count)
            outgoing.append(summed.reshape(TRACE_ROWS, SHOTS).astype(jnp.bfloat16))
        incoming = jnp.stack(outgoing)
        layers_out.append(incoming)
    return jnp.stack(layers_out)
```

```python
import functools

import jax
import jax.numpy as jnp
from jax import lax
from jax.experimental import pallas as pl
from jax.experimental.pallas import tpu as pltpu
from jax.sharding import PartitionSpec as P

MESH = pl.DeviceIdType.MESH
CHUNK = 16
PIECES = 2


def displacements(senders):
    side = 4 if senders == 32 else 2
    if side == 2:
        steps = [(1, 1), (1, 0), (0, 1)]
    else:
        steps = [(2, 2)]
        steps += [(2, 1), (1, 2), (2, 3), (3, 2)]
        steps += [(1, 1), (3, 1), (3, 3), (1, 3)]
        steps += [(2, 0), (0, 2)]
        steps += [(1, 0), (0, 1), (3, 0), (0, 3)]
    order, seen = [], set()
    for a, b in steps:
        kind = tuple(sorted((min(a, side - a), min(b, side - b))))
        if kind in seen:
            continue
        seen.add(kind)
        alike = [s for s in steps if tuple(sorted((min(s[0], side - s[0]), min(s[1], side - s[1])))) == kind]
        order += [(p, q, core) for core in range(2) for p, q in alike]
    return side, order + [(0, 0, 1)]


def sweep(
    side, order, table, operators, sources, out, blocks, field, sent, got, incoming,
    load_sem, send_sem, recv_sem, down_sem, arrive_sem,
):
    chunks, wide, rows = sources.shape
    stored, width, _ = blocks.shape
    owned = rows // width
    peers = len(order)
    part = owned // PIECES
    depth = lax.axis_index("layer")
    layers = lax.axis_size("layer")
    me = lax.axis_index("trace")
    z, y, core = me // (2 * side), (me // 2) % side, me % 2

    def at(step, sign):
        a, b, c = step
        return ((z + sign * a + side) % side) * (2 * side) + ((y + sign * b + side) % side) * 2 + (core + c) % 2

    load = pltpu.make_async_copy(operators, blocks, load_sem)
    load.start()
    barrier = pltpu.get_barrier_semaphore()
    for step in order:
        pl.semaphore_signal(barrier, inc=1, device_id=(depth, at(step, -1)), device_id_type=MESH)

    pl.semaphore_signal(
        barrier, inc=1, device_id=(lax.rem(depth + layers - 1, layers), me), device_id_type=MESH
    )
    pl.semaphore_wait(barrier, peers + 1)
    load.wait()

    def to_peer(k, i):
        return pltpu.make_async_remote_copy(
            src_ref=sent.at[k, i], dst_ref=got.at[k, i], send_sem=send_sem.at[k], recv_sem=recv_sem.at[k],
            device_id=(depth, at(order[i], 1)), device_id_type=MESH,
        )

    def all_peers(k):
        return pltpu.make_async_remote_copy(
            src_ref=sent.at[k], dst_ref=got.at[k, pl.ds(0, peers)], send_sem=send_sem.at[k],
            recv_sem=recv_sem.at[k], device_id=(depth, at(order[0], 1)), device_id_type=MESH,
        )

    def down(k, p):
        span = pl.ds(p * part * width, part * width)
        return pltpu.make_async_remote_copy(
            src_ref=out.at[k, :, span], dst_ref=incoming.at[k, :, span], send_sem=down_sem.at[k, p],
            recv_sem=arrive_sem.at[k, p], device_id=(lax.rem(depth + 1, layers), me), device_id_type=MESH,
        )

    def multiply(k):
        @pl.when(depth > 0)
        def _():
            for p in range(PIECES):
                down(k, p).wait_recv()

        for c in range(owned):
            span = pl.ds(c * width, width)
            above = jnp.where(depth > 0, incoming[k, :, span].astype(jnp.float32), 0.0)
            field[c] = (above + sources[k, :, span].astype(jnp.float32)).astype(jnp.bfloat16)
        for i in range(peers + 1):
            owner = at(order[i], 1) if i < peers else me
            product = lax.dot_general(
                field[table[1, owner]], blocks[table[0, owner]], (((1,), (1,)), ((), ())),
                preferred_element_type=jnp.float32,
            ).astype(jnp.bfloat16)
            if i < peers:
                sent[k, i] = product
                to_peer(k, i).start()
            else:
                got[k, i] = product

    def collect(k):
        all_peers(k).wait_recv()
        local = [table[2, at(order[i], -1) if i < peers else me] for i in range(peers + 1)]
        for p in range(PIECES):
            for r in range(p * part, (p + 1) * part):
                total = jnp.zeros((wide, width), jnp.float32)
                for i in range(peers + 1):
                    pick = jnp.where(local[i] == r, 1.0, 0.0)
                    total += got[k, i].astype(jnp.float32) * pick
                out[k, :, pl.ds(r * width, width)] = total.astype(jnp.bfloat16)

            @pl.when(depth < layers - 1)
            def _():
                down(k, p).start()

    def turn(k, _):
        @pl.when(k < chunks)
        def _():
            multiply(k)

        @pl.when(k > 0)
        def _():
            collect(k - 1)

        return 0

    lax.fori_loop(0, chunks + 1, turn, 0)

    def finish(k, _):
        all_peers(k).wait_send()

        @pl.when(depth < layers - 1)
        def _():
            for p in range(PIECES):
                down(k, p).wait_send()

        return 0

    lax.fori_loop(0, chunks, finish, 0)


def body(operators, sources, row_block, col_block):
    position = lax.axis_index("trace")
    senders = lax.axis_size("trace")
    blocks = operators[0]
    stored, width, _ = blocks.shape
    batches, rows, shots = sources.shape[1:]
    owned = rows // width
    side, order = displacements(senders)
    every = row_block[0]
    my_rows = lax.dynamic_index_in_dim(every, position, 0, keepdims=False)
    my_cols = col_block[0, 0] - position * owned
    match = (my_rows // owned)[None, :] == jnp.arange(senders)[:, None]
    slot = jnp.sum(jnp.where(match, jnp.arange(stored)[None, :], 0), axis=1)
    column = jnp.sum(jnp.where(match, my_cols[None, :], 0), axis=1)
    mine = every // owned == position
    local = jnp.sum(jnp.where(mine, every % owned + 1, 0), axis=1) - 1
    table = jnp.stack([slot, column, local]).astype(jnp.int32)
    chunks = batches * shots // CHUNK
    turned = jnp.swapaxes(sources[0], 1, 2).reshape(chunks, CHUNK, rows)
    peers = len(order)
    result = pl.pallas_call(
        functools.partial(sweep, side, order),
        out_shape=jax.ShapeDtypeStruct((chunks, CHUNK, rows), jnp.bfloat16),
        in_specs=[
            pl.BlockSpec(memory_space=pltpu.SMEM),
            pl.BlockSpec(memory_space=pl.ANY),
            pl.BlockSpec(memory_space=pltpu.VMEM),
        ],
        out_specs=pl.BlockSpec(memory_space=pltpu.VMEM),
        scratch_shapes=[
            pltpu.VMEM((stored, width, width), jnp.bfloat16),
            pltpu.VMEM((owned, CHUNK, width), jnp.bfloat16),
            pltpu.VMEM((chunks, peers, CHUNK, width), jnp.bfloat16),
            pltpu.VMEM((chunks, peers + 1, CHUNK, width), jnp.bfloat16),
            pltpu.VMEM((chunks, CHUNK, rows), jnp.bfloat16),
            pltpu.SemaphoreType.DMA,
            pltpu.SemaphoreType.DMA((chunks,)),
            pltpu.SemaphoreType.DMA((chunks,)),
            pltpu.SemaphoreType.DMA((chunks, PIECES)),
            pltpu.SemaphoreType.DMA((chunks, PIECES)),
        ],
        compiler_params=pltpu.CompilerParams(
            collective_id=0, has_side_effects=True, vmem_limit_bytes=56 * 1024 * 1024
        ),
        name="sweep",
    )(table, blocks, turned)
    return jnp.swapaxes(result.reshape(batches, shots, rows), 1, 2)[None]


def solution(mesh):
    placed = (
        P("layer", "trace", None, None),
        P("layer", None, "trace", None),
        P("layer", None, None),
        P("layer", "trace", None),
    )
    return jax.shard_map(
        body, mesh=mesh, in_specs=placed, out_specs=P("layer", None, "trace", None), check_vma=False
    )
```

```python
import functools

import jax
import jax.numpy as jnp
from jax import lax
from jax.experimental import pallas as pl
from jax.experimental.pallas import tpu as pltpu
from jax.sharding import PartitionSpec as P

MESH = pl.DeviceIdType.MESH
CHUNK = 16
PIECES = 4
LOADS = 6
RING = 4
GROUP = 4


def displacements(senders):
    side = 4 if senders == 32 else 2
    if side == 2:
        kinds = [[(1, 1)], [(1, 0), (0, 1)]]
    else:
        kinds = [
            [(2, 2)],
            [(2, 1), (1, 2), (2, 3), (3, 2)],
            [(1, 1), (3, 1), (3, 3), (1, 3)],
            [(2, 0), (0, 2)],
            [(1, 0), (0, 1), (3, 0), (0, 3)],
        ]
    order = [(a, b, core) for alike in kinds for core in range(2) for a, b in alike]
    return side, order + [(0, 0, 1)]


def sweep(
    side, order, row_block, col_block, operators, sources, result,
    raw, blocks, given, turned, field, sent, got, incoming, out, final, table_v, table,
    load_sem, given_sem, table_sem, result_sem, send_sem, recv_sem, down_sem, arrive_sem,
):
    chunks, wide, rows = incoming.shape
    stored, width, _ = blocks.shape
    batches, _, shots = given.shape
    each = chunks // batches
    owned = rows // width
    peers = len(order)
    part = owned // PIECES
    per_load = stored // LOADS
    depth = lax.axis_index("layer")
    layers = lax.axis_size("layer")
    me = lax.axis_index("trace")
    z, y, core = me // (2 * side), (me // 2) % side, me % 2

    def at(step, sign):
        a, b, c = step
        return ((z + sign * a + side) % side) * (2 * side) + ((y + sign * b + side) % side) * 2 + (core + c) % 2

    loads = [
        pltpu.make_async_copy(
            operators.at[pl.ds(g * per_load, per_load)], raw.at[pl.ds(g * per_load, per_load)], load_sem.at[g]
        )
        for g in range(LOADS)
    ]
    takes = [pltpu.make_async_copy(sources.at[b], given.at[b], given_sem.at[b]) for b in range(batches)]
    takes[0].start()
    for load in loads:
        load.start()
    for take in takes[1:]:
        take.start()
    barrier = pltpu.get_barrier_semaphore()
    for step in order:
        pl.semaphore_signal(barrier, inc=1, device_id=(depth, at(step, -1)), device_id_type=MESH)
    pl.semaphore_signal(
        barrier, inc=1, device_id=(lax.rem(depth + layers - 1, layers), me), device_id_type=MESH
    )

    every = row_block[...]
    mine = row_block[pl.ds(me, 1), :]
    senders = every.shape[0]
    owner = lax.broadcasted_iota(jnp.int32, every.shape, 0)
    match = jnp.broadcast_to(mine // owned, every.shape) == owner
    order_of = lax.broadcasted_iota(jnp.int32, every.shape, 1)
    near = jnp.broadcast_to(col_block[...] % owned, every.shape)
    slot = jnp.max(jnp.where(match, order_of, 0), axis=1, keepdims=True)
    column = jnp.max(jnp.where(match, near, 0), axis=1, keepdims=True)
    local = jnp.max(jnp.where(every // owned == me, every % owned + 1, 0), axis=1, keepdims=True) - 1
    lane = lax.broadcasted_iota(jnp.int32, table_v.shape, 1)
    table_v[...] = jnp.where(lane == 0, slot, jnp.where(lane == 1, column, local))
    to_scalars = pltpu.make_async_copy(table_v, table, table_sem)
    to_scalars.start()

    def turn_sources(b):
        for r in range(owned):
            span = pl.ds(r * width, width)
            turned[b, :, span] = given[b, span, :].T

    takes[0].wait()
    turn_sources(0)
    for g in range(LOADS):
        loads[g].wait()

        def flip(j, _):
            blocks[j] = raw[j].T
            return 0

        lax.fori_loop(g * per_load, (g + 1) * per_load, flip, 0)
    to_scalars.wait()
    for take in takes[1:]:
        take.wait()
    pl.semaphore_wait(barrier, peers + 1)

    def to_peer(k, i):
        return pltpu.make_async_remote_copy(
            src_ref=sent.at[k % RING, i], dst_ref=got.at[k, i], send_sem=send_sem.at[k], recv_sem=recv_sem.at[k],
            device_id=(depth, at(order[i], 1)), device_id_type=MESH,
        )

    def all_peers(k):
        return pltpu.make_async_remote_copy(
            src_ref=sent.at[k % RING], dst_ref=got.at[k, pl.ds(0, peers)], send_sem=send_sem.at[k],
            recv_sem=recv_sem.at[k], device_id=(depth, at(order[0], 1)), device_id_type=MESH,
        )

    def down(k, p):
        span = pl.ds(p * part * width, part * width)
        return pltpu.make_async_remote_copy(
            src_ref=out.at[k, :, span], dst_ref=incoming.at[k, :, span], send_sem=down_sem.at[k, p],
            recv_sem=arrive_sem.at[k, p], device_id=(lax.rem(depth + 1, layers), me), device_id_type=MESH,
        )

    def multiply(k):
        @pl.when(k >= RING)
        def _():
            all_peers(k - RING).wait_send()

        for b in range(1, batches):

            @pl.when(k == (b - 1) * each + 1)
            def _():
                turn_sources(b)

        shot = pl.ds(pl.multiple_of((k % each) * wide, wide), wide)
        for p in range(PIECES):

            @pl.when(depth > 0)
            def _():
                down(k, p).wait_recv()

            for c in range(p * part, (p + 1) * part):
                span = pl.ds(c * width, width)
                above = jnp.where(depth > 0, incoming[k, :, span].astype(jnp.float32), 0.0)
                field[c] = (above + turned[k // each, shot, span].astype(jnp.float32)).astype(jnp.bfloat16)
        for first in range(0, peers + 1, GROUP):
            span = range(first, min(first + GROUP, peers + 1))
            for i in span:
                owner = at(order[i], 1) if i < peers else me
                product = jnp.dot(
                    field[table[owner, 1]], blocks[table[owner, 0]], preferred_element_type=jnp.float32
                ).astype(jnp.bfloat16)
                if i < peers:
                    sent[k % RING, i] = product
                else:
                    got[k, i] = product
            for i in span:
                if i < peers:
                    to_peer(k, i).start()

    def collect(k):
        all_peers(k).wait_recv()
        local = [table[at(order[i], -1) if i < peers else me, 2] for i in range(peers + 1)]
        for p in range(PIECES):
            spread = range(p * part, (p + 1) * part)
            totals = [jnp.zeros((wide, width), jnp.float32) for _ in spread]
            for i in range(peers + 1):
                value = got[k, i].astype(jnp.float32)
                for n, r in enumerate(spread):
                    totals[n] += value * jnp.where(local[i] == r, 1.0, 0.0)
            for n, r in enumerate(spread):
                out[k, :, pl.ds(r * width, width)] = totals[n].astype(jnp.bfloat16)

            @pl.when(depth < layers - 1)
            def _():
                down(k, p).start()

    def hand_over(b):
        for r in range(owned):
            span = pl.ds(r * width, width)
            shots_all = out[pl.ds(b * each, each), :, span].reshape(shots, width)
            final[b, span, :] = shots_all.T
            pltpu.make_async_copy(final.at[b, span], result.at[b, span], result_sem.at[b]).start()

    def turn(k, _):
        @pl.when(k < chunks)
        def _():
            multiply(k)

        @pl.when(k > 0)
        def _():
            collect(k - 1)

        for b in range(batches):

            @pl.when(k == (b + 1) * each)
            def _():
                hand_over(b)

        return 0

    lax.fori_loop(0, chunks + 1, turn, 0)

    def finish(k, _):
        @pl.when(k >= chunks - RING)
        def _():
            all_peers(k).wait_send()

        @pl.when(depth < layers - 1)
        def _():
            for p in range(PIECES):
                down(k, p).wait_send()

        return 0

    lax.fori_loop(0, chunks, finish, 0)
    for b in range(batches):
        pltpu.make_async_copy(final.at[b], result.at[b], result_sem.at[b]).wait()


def body(operators, sources, row_block, col_block):
    senders = lax.axis_size("trace")
    _, stored, width, _ = operators.shape
    batches, rows, shots = sources.shape[1:]
    owned = rows // width
    side, order = displacements(senders)
    chunks = batches * shots // CHUNK
    peers = len(order)
    result = pl.pallas_call(
        functools.partial(sweep, side, order),
        out_shape=jax.ShapeDtypeStruct((batches, rows, shots), jnp.bfloat16),
        in_specs=[
            pl.BlockSpec(memory_space=pltpu.VMEM),
            pl.BlockSpec(memory_space=pltpu.VMEM),
            pl.BlockSpec(memory_space=pl.ANY),
            pl.BlockSpec(memory_space=pl.ANY),
        ],
        out_specs=pl.BlockSpec(memory_space=pl.ANY),
        scratch_shapes=[
            pltpu.VMEM((stored, width, width), jnp.bfloat16),
            pltpu.VMEM((stored, width, width), jnp.bfloat16),
            pltpu.VMEM((batches, rows, shots), jnp.bfloat16),
            pltpu.VMEM((batches, shots, rows), jnp.bfloat16),
            pltpu.VMEM((owned, CHUNK, width), jnp.bfloat16),
            pltpu.VMEM((RING, peers, CHUNK, width), jnp.bfloat16),
            pltpu.VMEM((chunks, peers + 1, CHUNK, width), jnp.bfloat16),
            pltpu.VMEM((chunks, CHUNK, rows), jnp.bfloat16),
            pltpu.VMEM((chunks, CHUNK, rows), jnp.bfloat16),
            pltpu.VMEM((batches, rows, shots), jnp.bfloat16),
            pltpu.VMEM((senders, 128), jnp.int32),
            pltpu.SMEM((senders, 128), jnp.int32),
            pltpu.SemaphoreType.DMA((LOADS,)),
            pltpu.SemaphoreType.DMA((batches,)),
            pltpu.SemaphoreType.DMA,
            pltpu.SemaphoreType.DMA((batches,)),
            pltpu.SemaphoreType.DMA((chunks,)),
            pltpu.SemaphoreType.DMA((chunks,)),
            pltpu.SemaphoreType.DMA((chunks, PIECES)),
            pltpu.SemaphoreType.DMA((chunks, PIECES)),
        ],
        compiler_params=pltpu.CompilerParams(
            collective_id=0, has_side_effects=True, vmem_limit_bytes=58 * 1024 * 1024
        ),
        name="sweep",
    )(row_block[0], col_block[0], operators[0], sources[0])
    return result[None]


def solution(mesh):
    placed = (
        P("layer", "trace", None, None),
        P("layer", None, "trace", None),
        P("layer", None, None),
        P("layer", "trace", None),
    )
    return jax.shard_map(
        body, mesh=mesh, in_specs=placed, out_specs=P("layer", None, "trace", None), check_vma=False
    )
```

```python
import functools

import jax
import jax.numpy as jnp
from jax import lax
from jax.experimental import pallas as pl
from jax.experimental.pallas import tpu as pltpu
from jax.sharding import PartitionSpec as P

MESH = pl.DeviceIdType.MESH
CHUNK = 8
PIECES = 2
LOADS = 6
RING = 6
GROUP = 4


def displacements(senders):
    side = 4 if senders == 32 else 2
    if side == 2:
        kinds = [[(1, 1)], [(1, 0), (0, 1)]]
    else:
        kinds = [
            [(2, 2)],
            [(2, 1), (1, 2), (2, 3), (3, 2)],
            [(1, 1), (3, 1), (3, 3), (1, 3)],
            [(2, 0), (0, 2)],
            [(1, 0), (0, 1), (3, 0), (0, 3)],
        ]
    order = [(a, b, core) for alike in kinds for core in range(2) for a, b in alike]
    return side, order + [(0, 0, 1)]


def fold(values):
    half = values.shape[1] // 2
    return jnp.concatenate([values[:, :half], values[:, half:]], axis=0)


def unfold(values):
    half = values.shape[0] // 2
    return jnp.concatenate([values[:half], values[half:]], axis=1)


def sweep(
    side, order, row_block, col_block, operators, sources, result,
    raw, blocks, turned, field, products, sent, got, incoming, out, whole, table_v, table,
    load_sem, table_sem, send_sem, recv_sem, down_sem, arrive_sem,
):
    chunks = incoming.shape[0]
    stored, width, _ = blocks.shape
    batches, rows, shots = sources.shape
    wide = batches * shots // chunks
    half = width // 2
    each = chunks // batches
    owned = rows // width
    peers = len(order)
    part = owned // PIECES
    per_load = stored // LOADS
    depth = lax.axis_index("layer")
    layers = lax.axis_size("layer")
    me = lax.axis_index("trace")
    z, y, core = me // (2 * side), (me // 2) % side, me % 2

    def at(step, sign):
        a, b, c = step
        return ((z + sign * a + side) % side) * (2 * side) + ((y + sign * b + side) % side) * 2 + (core + c) % 2

    loads = [
        pltpu.make_async_copy(
            operators.at[pl.ds(g * per_load, per_load)], raw.at[pl.ds(g * per_load, per_load)], load_sem.at[g]
        )
        for g in range(LOADS)
    ]
    for load in loads:
        load.start()
    barrier = pltpu.get_barrier_semaphore()
    for step in order:
        pl.semaphore_signal(barrier, inc=1, device_id=(depth, at(step, -1)), device_id_type=MESH)
    pl.semaphore_signal(
        barrier, inc=1, device_id=(lax.rem(depth + layers - 1, layers), me), device_id_type=MESH
    )

    every = row_block[...]
    shape = every.shape
    place = lax.broadcasted_iota(jnp.int32, shape, 0)
    index = lax.broadcasted_iota(jnp.int32, shape, 1)
    mine = jnp.sum(jnp.where(index == me, every, 0), axis=1, keepdims=True)
    square = (stored, stored)
    diagonal = lax.broadcasted_iota(jnp.int32, square, 0) == lax.broadcasted_iota(jnp.int32, square, 1)
    near = jnp.sum(jnp.where(diagonal, col_block[...] % owned, 0), axis=1, keepdims=True)
    match = mine // owned == index
    slot = jnp.max(jnp.where(match, place, 0), axis=0, keepdims=True)
    column = jnp.max(jnp.where(match, near, 0), axis=0, keepdims=True)
    local = jnp.max(jnp.where(every // owned == me, every % owned + 1, 0), axis=0, keepdims=True) - 1
    table_v[0:1, 0 : shape[1]] = slot
    table_v[1:2, 0 : shape[1]] = column
    table_v[2:3, 0 : shape[1]] = local
    table_v[3:4, 0:stored] = col_block[...] % owned
    to_scalars = pltpu.make_async_copy(table_v, table, table_sem)
    to_scalars.start()

    def turn_sources(b):
        for r in range(owned):
            span = pl.ds(r * width, width)
            turned[b, :, span] = sources[b, span, :].astype(jnp.float32).T

    turn_sources(0)
    for g in range(LOADS):
        loads[g].wait()

        def flip(j, _):
            blocks[j] = raw[j].T
            return 0

        lax.fori_loop(g * per_load, (g + 1) * per_load, flip, 0)
    to_scalars.wait()
    pl.semaphore_wait(barrier, peers + 1)

    def to_peer(k, i):
        return pltpu.make_async_remote_copy(
            src_ref=sent.at[k % RING, i], dst_ref=got.at[k, i], send_sem=send_sem.at[k], recv_sem=recv_sem.at[k],
            device_id=(depth, at(order[i], 1)), device_id_type=MESH,
        )

    def all_peers(k):
        return pltpu.make_async_remote_copy(
            src_ref=sent.at[k % RING], dst_ref=got.at[k, pl.ds(0, peers)], send_sem=send_sem.at[k],
            recv_sem=recv_sem.at[k], device_id=(depth, at(order[0], 1)), device_id_type=MESH,
        )

    def down(k, p):
        span = pl.ds(p * part * half, part * half)
        return pltpu.make_async_remote_copy(
            src_ref=out.at[k, :, span], dst_ref=incoming.at[k, :, span], send_sem=down_sem.at[k, p],
            recv_sem=arrive_sem.at[k, p], device_id=(lax.rem(depth + 1, layers), me), device_id_type=MESH,
        )

    def multiply(k):
        @pl.when(k >= RING)
        def _():
            all_peers(k - RING).wait_send()

        for b in range(1, batches):

            @pl.when(k == (b - 1) * each + 1)
            def _():
                turn_sources(b)

        shot = pl.ds(pl.multiple_of((k % each) * wide, wide), wide)
        for p in range(PIECES):

            @pl.when(depth > 0)
            def _():
                down(k, p).wait_recv()

            for c in range(p * part, (p + 1) * part):
                above = unfold(incoming[k, :, pl.ds(c * half, half)].astype(jnp.float32))
                tile = jnp.where(depth > 0, above, 0.0) + turned[k // each, shot, pl.ds(c * width, width)]
                field[c] = jnp.concatenate([tile, tile], axis=0).astype(jnp.bfloat16)
        for j in range(stored):
            product = jnp.dot(field[table[3, j]], blocks[j], preferred_element_type=jnp.float32)
            products[j] = fold(product[:wide]).astype(jnp.bfloat16)
        for first in range(0, peers + 1, GROUP):
            span = range(first, min(first + GROUP, peers + 1))
            for i in span:
                owner = at(order[i], 1) if i < peers else me
                if i < peers:
                    sent[k % RING, i] = products[table[0, owner]]
                else:
                    got[k, i] = products[table[0, owner]]
            for i in span:
                if i < peers:
                    to_peer(k, i).start()

    def collect(k):
        all_peers(k).wait_recv()
        shot = pl.ds(pl.multiple_of((k % each) * wide, wide), wide)
        local = [table[2, at(order[i], -1) if i < peers else me] for i in range(peers + 1)]
        for p in range(PIECES):
            spread = range(p * part, (p + 1) * part)
            totals = [jnp.zeros((2 * wide, half), jnp.float32) for _ in spread]
            for i in range(peers + 1):
                value = got[k, i].astype(jnp.float32)
                for n, r in enumerate(spread):
                    totals[n] += value * jnp.where(local[i] == r, 1.0, 0.0)
            for n, r in enumerate(spread):
                out[k, :, pl.ds(r * half, half)] = totals[n].astype(jnp.bfloat16)
                whole[shot, pl.ds(r * width, width)] = unfold(totals[n])

            @pl.when(depth < layers - 1)
            def _():
                down(k, p).start()

    def hand_over(b):
        for r in range(owned):
            span = pl.ds(r * width, width)
            result[b, span, :] = whole[:, span].T.astype(jnp.bfloat16)

    behind = jnp.where(depth == 0, 3, 2)

    def turn(k, _):
        @pl.when(k < chunks)
        def _():
            multiply(k)

        done = k - behind

        @pl.when((done >= 0) & (done < chunks))
        def _():
            collect(done)

        for b in range(batches):

            @pl.when(done == (b + 1) * each - 1)
            def _():
                hand_over(b)

        return 0

    lax.fori_loop(0, chunks + 3, turn, 0)

    def finish(k, _):
        @pl.when(k >= chunks - RING)
        def _():
            all_peers(k).wait_send()

        @pl.when(depth < layers - 1)
        def _():
            for p in range(PIECES):
                down(k, p).wait_send()

        return 0

    lax.fori_loop(0, chunks, finish, 0)


def body(operators, sources, row_block, col_block):
    senders = lax.axis_size("trace")
    _, stored, width, _ = operators.shape
    batches, rows, shots = sources.shape[1:]
    owned = rows // width
    side, order = displacements(senders)
    chunks = batches * shots // CHUNK
    peers = len(order)
    result = pl.pallas_call(
        functools.partial(sweep, side, order),
        out_shape=jax.ShapeDtypeStruct((batches, rows, shots), jnp.bfloat16),
        in_specs=[
            pl.BlockSpec(memory_space=pltpu.VMEM),
            pl.BlockSpec(memory_space=pltpu.VMEM),
            pl.BlockSpec(memory_space=pl.ANY),
            pl.BlockSpec(memory_space=pltpu.VMEM),
        ],
        out_specs=pl.BlockSpec(memory_space=pltpu.VMEM),
        scratch_shapes=[
            pltpu.VMEM((stored, width, width), jnp.bfloat16),
            pltpu.VMEM((stored, width, width), jnp.bfloat16),
            pltpu.VMEM((batches, shots, rows), jnp.float32),
            pltpu.VMEM((owned, 2 * CHUNK, width), jnp.bfloat16),
            pltpu.VMEM((stored, 2 * CHUNK, width // 2), jnp.bfloat16),
            pltpu.VMEM((RING, peers, 2 * CHUNK, width // 2), jnp.bfloat16),
            pltpu.VMEM((chunks, peers + 1, 2 * CHUNK, width // 2), jnp.bfloat16),
            pltpu.VMEM((chunks, 2 * CHUNK, rows // 2), jnp.bfloat16),
            pltpu.VMEM((chunks, 2 * CHUNK, rows // 2), jnp.bfloat16),
            pltpu.VMEM((shots, rows), jnp.float32),
            pltpu.VMEM((8, 128), jnp.int32),
            pltpu.SMEM((8, 128), jnp.int32),
            pltpu.SemaphoreType.DMA((LOADS,)),
            pltpu.SemaphoreType.DMA,
            pltpu.SemaphoreType.DMA((chunks,)),
            pltpu.SemaphoreType.DMA((chunks,)),
            pltpu.SemaphoreType.DMA((chunks, PIECES)),
            pltpu.SemaphoreType.DMA((chunks, PIECES)),
        ],
        compiler_params=pltpu.CompilerParams(
            collective_id=0, has_side_effects=True, vmem_limit_bytes=54 * 1024 * 1024
        ),
        name="sweep",
    )(row_block[0].T, col_block[0], operators[0], sources[0])
    return result[None]


def solution(mesh):
    placed = (
        P("layer", "trace", None, None),
        P("layer", None, "trace", None),
        P("layer", None, None),
        P("layer", "trace", None),
    )
    return jax.shard_map(
        body, mesh=mesh, in_specs=placed, out_specs=P("layer", None, "trace", None), check_vma=False
    )
```

```python
import functools

import jax
import jax.numpy as jnp
from jax import lax
from jax.experimental import pallas as pl
from jax.experimental.pallas import tpu as pltpu
from jax.sharding import PartitionSpec as P

MESH = pl.DeviceIdType.MESH
CHUNK = 8
PIECES = 2
LOADS = 6
RING = 6
EARLY = 4
GROUP = 4


def displacements(senders):
    side = 4 if senders == 32 else 2
    if side == 2:
        kinds = [[(1, 1)], [(1, 0), (0, 1)]]
    else:
        kinds = [
            [(2, 2)],
            [(2, 1), (1, 2), (2, 3), (3, 2)],
            [(1, 1), (3, 1), (3, 3), (1, 3)],
            [(2, 0), (0, 2)],
            [(1, 0), (0, 1), (3, 0), (0, 3)],
        ]
    order = [(a, b, core) for alike in kinds for core in range(2) for a, b in alike]
    return side, order + [(0, 0, 1)]


def fold(values):
    half = values.shape[1] // 2
    return jnp.concatenate([values[:, :half], values[:, half:]], axis=0)


def unfold(values):
    half = values.shape[0] // 2
    return jnp.concatenate([values[:half], values[half:]], axis=1)


def sweep(
    side, order, row_block, col_block, operators, sources, result,
    raw, blocks, turned, ahead, first, field, products, sent, got, incoming, out, whole, table_v, table,
    load_sem, table_sem, send_sem, recv_sem, down_sem, arrive_sem,
):
    chunks = incoming.shape[0]
    stored, width, _ = blocks.shape
    batches, rows, shots = sources.shape
    wide = batches * shots // chunks
    half = width // 2
    each = chunks // batches
    owned = rows // width
    peers = len(order)
    part = owned // PIECES
    per_load = stored // LOADS
    depth = lax.axis_index("layer")
    layers = lax.axis_size("layer")
    me = lax.axis_index("trace")
    z, y, core = me // (2 * side), (me // 2) % side, me % 2

    def at(step, sign):
        a, b, c = step
        return ((z + sign * a + side) % side) * (2 * side) + ((y + sign * b + side) % side) * 2 + (core + c) % 2

    loads = [
        pltpu.make_async_copy(
            operators.at[pl.ds(g * per_load, per_load)], raw.at[pl.ds(g * per_load, per_load)], load_sem.at[g]
        )
        for g in range(LOADS)
    ]
    for load in loads:
        load.start()
    barrier = pltpu.get_barrier_semaphore()
    for step in order:
        pl.semaphore_signal(barrier, inc=1, device_id=(depth, at(step, -1)), device_id_type=MESH)
    pl.semaphore_signal(
        barrier, inc=1, device_id=(lax.rem(depth + layers - 1, layers), me), device_id_type=MESH
    )

    every = row_block[...]
    shape = every.shape
    place = lax.broadcasted_iota(jnp.int32, shape, 0)
    index = lax.broadcasted_iota(jnp.int32, shape, 1)
    mine = jnp.sum(jnp.where(index == me, every, 0), axis=1, keepdims=True)
    square = (stored, stored)
    diagonal = lax.broadcasted_iota(jnp.int32, square, 0) == lax.broadcasted_iota(jnp.int32, square, 1)
    near = jnp.sum(jnp.where(diagonal, col_block[...] % owned, 0), axis=1, keepdims=True)
    match = mine // owned == index
    slot = jnp.max(jnp.where(match, place, 0), axis=0, keepdims=True)
    column = jnp.max(jnp.where(match, near, 0), axis=0, keepdims=True)
    local = jnp.max(jnp.where(every // owned == me, every % owned + 1, 0), axis=0, keepdims=True) - 1
    table_v[0:1, 0 : shape[1]] = slot
    table_v[1:2, 0 : shape[1]] = column
    table_v[2:3, 0 : shape[1]] = local
    table_v[3:4, 0:stored] = col_block[...] % owned
    to_scalars = pltpu.make_async_copy(table_v, table, table_sem)
    to_scalars.start()

    def turn_sources(b):
        for r in range(owned):
            span = pl.ds(r * width, width)
            turned[b, :, span] = sources[b, span, :].astype(jnp.float32).T

    def early(g):
        for j in range(g * per_load, (g + 1) * per_load):
            column = table[3, j]
            product = lax.dot_general(
                ahead[column], raw[j], (((1,), (1,)), ((), ())), preferred_element_type=jnp.float32
            )
            for k in range(EARLY):
                first[k, j] = fold(product[k * wide : (k + 1) * wide]).astype(jnp.bfloat16)

    def flip_all():
        def flip(j, _):
            blocks[j] = raw[j].T
            return 0

        lax.fori_loop(0, stored, flip, 0)

    turn_sources(0)
    for c in range(owned):
        ahead[c] = turned[0, 0 : EARLY * wide, pl.ds(c * width, width)].astype(jnp.bfloat16)
    to_scalars.wait()
    for g in range(LOADS):
        loads[g].wait()

        @pl.when(depth == 0)
        def _():
            early(g)

    pl.semaphore_wait(barrier, peers + 1)

    def to_peer(k, i):
        return pltpu.make_async_remote_copy(
            src_ref=sent.at[k % RING, i], dst_ref=got.at[k, i], send_sem=send_sem.at[k], recv_sem=recv_sem.at[k],
            device_id=(depth, at(order[i], 1)), device_id_type=MESH,
        )

    def all_peers(k):
        return pltpu.make_async_remote_copy(
            src_ref=sent.at[k % RING], dst_ref=got.at[k, pl.ds(0, peers)], send_sem=send_sem.at[k],
            recv_sem=recv_sem.at[k], device_id=(depth, at(order[0], 1)), device_id_type=MESH,
        )

    def down(k, p):
        span = pl.ds(p * part * half, part * half)
        return pltpu.make_async_remote_copy(
            src_ref=out.at[k, :, span], dst_ref=incoming.at[k, :, span], send_sem=down_sem.at[k, p],
            recv_sem=arrive_sem.at[k, p], device_id=(lax.rem(depth + 1, layers), me), device_id_type=MESH,
        )

    def send(k, held):
        for start in range(0, peers + 1, GROUP):
            span = range(start, min(start + GROUP, peers + 1))
            for i in span:
                owner = at(order[i], 1) if i < peers else me
                if i < peers:
                    sent[k % RING, i] = held[table[0, owner]]
                else:
                    got[k, i] = held[table[0, owner]]
            for i in span:
                if i < peers:
                    to_peer(k, i).start()

    def multiply(k):
        @pl.when(k >= RING)
        def _():
            all_peers(k - RING).wait_send()

        for b in range(1, batches):

            @pl.when(k == (b - 1) * each + EARLY + 1)
            def _():
                turn_sources(b)

        shot = pl.ds(pl.multiple_of((k % each) * wide, wide), wide)
        for p in range(PIECES):

            @pl.when(depth > 0)
            def _():
                down(k, p).wait_recv()

            for c in range(p * part, (p + 1) * part):
                above = unfold(incoming[k, :, pl.ds(c * half, half)].astype(jnp.float32))
                tile = jnp.where(depth > 0, above, 0.0) + turned[k // each, shot, pl.ds(c * width, width)]
                field[c] = jnp.concatenate([tile, tile], axis=0).astype(jnp.bfloat16)
        for j in range(stored):
            product = jnp.dot(field[table[3, j]], blocks[j], preferred_element_type=jnp.float32)
            products[j] = fold(product[:wide]).astype(jnp.bfloat16)
        send(k, products)

    def collect(k):
        all_peers(k).wait_recv()
        shot = pl.ds(pl.multiple_of((k % each) * wide, wide), wide)
        local = [table[2, at(order[i], -1) if i < peers else me] for i in range(peers + 1)]
        for p in range(PIECES):
            spread = range(p * part, (p + 1) * part)
            totals = [jnp.zeros((2 * wide, half), jnp.float32) for _ in spread]
            for i in range(peers + 1):
                value = got[k, i].astype(jnp.float32)
                for n, r in enumerate(spread):
                    totals[n] += value * jnp.where(local[i] == r, 1.0, 0.0)
            for n, r in enumerate(spread):
                out[k, :, pl.ds(r * half, half)] = totals[n].astype(jnp.bfloat16)
                whole[shot, pl.ds(r * width, width)] = unfold(totals[n])

            @pl.when(depth < layers - 1)
            def _():
                down(k, p).start()

    def hand_over(b):
        for r in range(owned):
            span = pl.ds(r * width, width)
            result[b, span, :] = whole[:, span].T.astype(jnp.bfloat16)

    @pl.when(depth == 0)
    def _():
        for k in range(EARLY):
            send(k, first.at[k])

    flip_all()
    behind = jnp.where(depth == 0, 3, 2)
    begin = jnp.where(depth == 0, EARLY, 0)

    def turn(k, _):
        @pl.when((k < chunks) & (k >= begin))
        def _():
            multiply(k)

        done = k - behind

        @pl.when((done >= 0) & (done < chunks))
        def _():
            collect(done)

        for b in range(batches):

            @pl.when(done == (b + 1) * each - 1)
            def _():
                hand_over(b)

        return 0

    lax.fori_loop(0, chunks + 3, turn, 0)

    def finish(k, _):
        @pl.when(k >= chunks - RING)
        def _():
            all_peers(k).wait_send()

        @pl.when(depth < layers - 1)
        def _():
            for p in range(PIECES):
                down(k, p).wait_send()

        return 0

    lax.fori_loop(0, chunks, finish, 0)


def body(operators, sources, row_block, col_block):
    senders = lax.axis_size("trace")
    _, stored, width, _ = operators.shape
    batches, rows, shots = sources.shape[1:]
    owned = rows // width
    side, order = displacements(senders)
    chunks = batches * shots // CHUNK
    peers = len(order)
    result = pl.pallas_call(
        functools.partial(sweep, side, order),
        out_shape=jax.ShapeDtypeStruct((batches, rows, shots), jnp.bfloat16),
        in_specs=[
            pl.BlockSpec(memory_space=pltpu.VMEM),
            pl.BlockSpec(memory_space=pltpu.VMEM),
            pl.BlockSpec(memory_space=pl.ANY),
            pl.BlockSpec(memory_space=pltpu.VMEM),
        ],
        out_specs=pl.BlockSpec(memory_space=pltpu.VMEM),
        scratch_shapes=[
            pltpu.VMEM((stored, width, width), jnp.bfloat16),
            pltpu.VMEM((stored, width, width), jnp.bfloat16),
            pltpu.VMEM((batches, shots, rows), jnp.float32),
            pltpu.VMEM((owned, EARLY * CHUNK, width), jnp.bfloat16),
            pltpu.VMEM((EARLY, stored, 2 * CHUNK, width // 2), jnp.bfloat16),
            pltpu.VMEM((owned, 2 * CHUNK, width), jnp.bfloat16),
            pltpu.VMEM((stored, 2 * CHUNK, width // 2), jnp.bfloat16),
            pltpu.VMEM((RING, peers, 2 * CHUNK, width // 2), jnp.bfloat16),
            pltpu.VMEM((chunks, peers + 1, 2 * CHUNK, width // 2), jnp.bfloat16),
            pltpu.VMEM((chunks, 2 * CHUNK, rows // 2), jnp.bfloat16),
            pltpu.VMEM((chunks, 2 * CHUNK, rows // 2), jnp.bfloat16),
            pltpu.VMEM((shots, rows), jnp.float32),
            pltpu.VMEM((8, 128), jnp.int32),
            pltpu.SMEM((8, 128), jnp.int32),
            pltpu.SemaphoreType.DMA((LOADS,)),
            pltpu.SemaphoreType.DMA,
            pltpu.SemaphoreType.DMA((chunks,)),
            pltpu.SemaphoreType.DMA((chunks,)),
            pltpu.SemaphoreType.DMA((chunks, PIECES)),
            pltpu.SemaphoreType.DMA((chunks, PIECES)),
        ],
        compiler_params=pltpu.CompilerParams(
            collective_id=0, has_side_effects=True, vmem_limit_bytes=50 * 1024 * 1024
        ),
        name="sweep",
    )(row_block[0].T, col_block[0], operators[0], sources[0])
    return result[None]


def solution(mesh):
    placed = (
        P("layer", "trace", None, None),
        P("layer", None, "trace", None),
        P("layer", None, None),
        P("layer", "trace", None),
    )
    return jax.shard_map(
        body, mesh=mesh, in_specs=placed, out_specs=P("layer", None, "trace", None), check_vma=False
    )
```

```python
import functools

import jax
import jax.numpy as jnp
from jax import lax
from jax.experimental import pallas as pl
from jax.experimental.pallas import tpu as pltpu
from jax.sharding import PartitionSpec as P

MESH = pl.DeviceIdType.MESH
CHUNK = 8
PIECES = 1
LOADS = 6
RING = 6
EARLY = 4
GROUP = 4


def displacements(senders):
    side = 4 if senders == 32 else 2
    if side == 2:
        kinds = [[(1, 1)], [(1, 0), (0, 1)]]
    else:
        kinds = [
            [(2, 2)],
            [(2, 1), (1, 2), (2, 3), (3, 2)],
            [(1, 1), (3, 1), (3, 3), (1, 3)],
            [(2, 0), (0, 2)],
            [(1, 0), (0, 1), (3, 0), (0, 3)],
        ]
    order = [(a, b, core) for alike in kinds for core in range(2) for a, b in alike]
    return side, order + [(0, 0, 1)]


def fold(values):
    half = values.shape[1] // 2
    return jnp.concatenate([values[:, :half], values[:, half:]], axis=0)


def unfold(values):
    half = values.shape[0] // 2
    return jnp.concatenate([values[:half], values[half:]], axis=1)


def sweep(
    side, order, row_block, col_block, operators, sources, result,
    raw, blocks, turned, ahead, first, field, products, sent, got, incoming, out, whole, table_v, table,
    load_sem, table_sem, send_sem, recv_sem, down_sem, arrive_sem,
):
    chunks = incoming.shape[0]
    stored, width, _ = blocks.shape
    batches, rows, shots = sources.shape
    wide = batches * shots // chunks
    half = width // 2
    each = chunks // batches
    owned = rows // width
    peers = len(order)
    part = owned // PIECES
    per_load = stored // LOADS
    depth = lax.axis_index("layer")
    layers = lax.axis_size("layer")
    me = lax.axis_index("trace")
    z, y, core = me // (2 * side), (me // 2) % side, me % 2

    def at(step, sign):
        a, b, c = step
        return ((z + sign * a + side) % side) * (2 * side) + ((y + sign * b + side) % side) * 2 + (core + c) % 2

    loads = [
        pltpu.make_async_copy(
            operators.at[pl.ds(g * per_load, per_load)], raw.at[pl.ds(g * per_load, per_load)], load_sem.at[g]
        )
        for g in range(LOADS)
    ]
    for load in loads:
        load.start()
    barrier = pltpu.get_barrier_semaphore()
    for step in order:
        pl.semaphore_signal(barrier, inc=1, device_id=(depth, at(step, -1)), device_id_type=MESH)
    pl.semaphore_signal(
        barrier, inc=1, device_id=(lax.rem(depth + layers - 1, layers), me), device_id_type=MESH
    )

    every = row_block[...]
    shape = every.shape
    place = lax.broadcasted_iota(jnp.int32, shape, 0)
    index = lax.broadcasted_iota(jnp.int32, shape, 1)
    mine = jnp.sum(jnp.where(index == me, every, 0), axis=1, keepdims=True)
    square = (stored, stored)
    diagonal = lax.broadcasted_iota(jnp.int32, square, 0) == lax.broadcasted_iota(jnp.int32, square, 1)
    near = jnp.sum(jnp.where(diagonal, col_block[...] % owned, 0), axis=1, keepdims=True)
    match = mine // owned == index
    slot = jnp.max(jnp.where(match, place, 0), axis=0, keepdims=True)
    column = jnp.max(jnp.where(match, near, 0), axis=0, keepdims=True)
    local = jnp.max(jnp.where(every // owned == me, every % owned + 1, 0), axis=0, keepdims=True) - 1
    table_v[0:1, 0 : shape[1]] = slot
    table_v[1:2, 0 : shape[1]] = column
    table_v[2:3, 0 : shape[1]] = local
    table_v[3:4, 0:stored] = col_block[...] % owned
    to_scalars = pltpu.make_async_copy(table_v, table, table_sem)
    to_scalars.start()

    def turn_sources(b):
        for r in range(owned):
            span = pl.ds(r * width, width)
            turned[b, :, span] = sources[b, span, :].astype(jnp.float32).T

    def early(g):
        for j in range(g * per_load, (g + 1) * per_load):
            column = table[3, j]
            product = lax.dot_general(
                ahead[column], raw[j], (((1,), (1,)), ((), ())), preferred_element_type=jnp.float32
            )
            for k in range(EARLY):
                first[k, j] = fold(product[k * wide : (k + 1) * wide]).astype(jnp.bfloat16)

    def flip_all():
        def flip(j, _):
            blocks[j] = raw[j].T
            return 0

        lax.fori_loop(0, stored, flip, 0)

    turn_sources(0)
    for c in range(owned):
        ahead[c] = turned[0, 0 : EARLY * wide, pl.ds(c * width, width)].astype(jnp.bfloat16)
    to_scalars.wait()
    for g in range(LOADS):
        loads[g].wait()

        @pl.when(depth == 0)
        def _():
            early(g)

    pl.semaphore_wait(barrier, peers + 1)

    def to_peer(k, i):
        return pltpu.make_async_remote_copy(
            src_ref=sent.at[k % RING, i], dst_ref=got.at[k, i], send_sem=send_sem.at[k], recv_sem=recv_sem.at[k],
            device_id=(depth, at(order[i], 1)), device_id_type=MESH,
        )

    def all_peers(k):
        return pltpu.make_async_remote_copy(
            src_ref=sent.at[k % RING], dst_ref=got.at[k, pl.ds(0, peers)], send_sem=send_sem.at[k],
            recv_sem=recv_sem.at[k], device_id=(depth, at(order[0], 1)), device_id_type=MESH,
        )

    def down(k, p):
        span = pl.ds(p * part * half, part * half)
        return pltpu.make_async_remote_copy(
            src_ref=out.at[k, :, span], dst_ref=incoming.at[k, :, span], send_sem=down_sem.at[k, p],
            recv_sem=arrive_sem.at[k, p], device_id=(lax.rem(depth + 1, layers), me), device_id_type=MESH,
        )

    def send(k, held):
        for start in range(0, peers + 1, GROUP):
            span = range(start, min(start + GROUP, peers + 1))
            for i in span:
                owner = at(order[i], 1) if i < peers else me
                if i < peers:
                    sent[k % RING, i] = held[table[0, owner]]
                else:
                    got[k, i] = held[table[0, owner]]
            for i in span:
                if i < peers:
                    to_peer(k, i).start()

    def multiply(k):
        @pl.when(k >= RING)
        def _():
            all_peers(k - RING).wait_send()

        for b in range(1, batches):

            @pl.when(k == (b - 1) * each + EARLY + 1)
            def _():
                turn_sources(b)

        shot = pl.ds(pl.multiple_of((k % each) * wide, wide), wide)
        for p in range(PIECES):

            @pl.when(depth > 0)
            def _():
                down(k, p).wait_recv()

            for c in range(p * part, (p + 1) * part):
                above = unfold(incoming[k, :, pl.ds(c * half, half)].astype(jnp.float32))
                tile = jnp.where(depth > 0, above, 0.0) + turned[k // each, shot, pl.ds(c * width, width)]
                field[c] = jnp.concatenate([tile, tile], axis=0).astype(jnp.bfloat16)
        for j in range(stored):
            product = jnp.dot(field[table[3, j]], blocks[j], preferred_element_type=jnp.float32)
            products[j] = fold(product[:wide]).astype(jnp.bfloat16)
        send(k, products)

    def collect(k):
        all_peers(k).wait_recv()
        shot = pl.ds(pl.multiple_of((k % each) * wide, wide), wide)
        local = [table[2, at(order[i], -1) if i < peers else me] for i in range(peers + 1)]
        for p in range(PIECES):
            spread = range(p * part, (p + 1) * part)
            totals = [jnp.zeros((2 * wide, half), jnp.float32) for _ in spread]
            for i in range(peers + 1):
                value = got[k, i].astype(jnp.float32)
                for n, r in enumerate(spread):
                    totals[n] += value * jnp.where(local[i] == r, 1.0, 0.0)
            for n, r in enumerate(spread):
                out[k, :, pl.ds(r * half, half)] = totals[n].astype(jnp.bfloat16)
                whole[shot, pl.ds(r * width, width)] = unfold(totals[n])

            @pl.when(depth < layers - 1)
            def _():
                down(k, p).start()

    def hand_over(b):
        for r in range(owned):
            span = pl.ds(r * width, width)
            result[b, span, :] = whole[:, span].T.astype(jnp.bfloat16)

    @pl.when(depth == 0)
    def _():
        for k in range(EARLY):
            send(k, first.at[k])

    flip_all()
    behind = jnp.where(depth == 0, 3, 2)
    begin = jnp.where(depth == 0, EARLY, 0)

    def turn(k, _):
        @pl.when((k < chunks) & (k >= begin))
        def _():
            multiply(k)

        done = k - behind

        @pl.when((done >= 0) & (done < chunks))
        def _():
            collect(done)

        for b in range(batches):

            @pl.when(done == (b + 1) * each - 1)
            def _():
                hand_over(b)

        return 0

    lax.fori_loop(0, chunks + 3, turn, 0)

    def finish(k, _):
        @pl.when(k >= chunks - RING)
        def _():
            all_peers(k).wait_send()

        @pl.when(depth < layers - 1)
        def _():
            for p in range(PIECES):
                down(k, p).wait_send()

        return 0

    lax.fori_loop(0, chunks, finish, 0)


def body(operators, sources, row_block, col_block):
    senders = lax.axis_size("trace")
    _, stored, width, _ = operators.shape
    batches, rows, shots = sources.shape[1:]
    owned = rows // width
    side, order = displacements(senders)
    chunks = batches * shots // CHUNK
    peers = len(order)
    result = pl.pallas_call(
        functools.partial(sweep, side, order),
        out_shape=jax.ShapeDtypeStruct((batches, rows, shots), jnp.bfloat16),
        in_specs=[
            pl.BlockSpec(memory_space=pltpu.VMEM),
            pl.BlockSpec(memory_space=pltpu.VMEM),
            pl.BlockSpec(memory_space=pl.ANY),
            pl.BlockSpec(memory_space=pltpu.VMEM),
        ],
        out_specs=pl.BlockSpec(memory_space=pltpu.VMEM),
        scratch_shapes=[
            pltpu.VMEM((stored, width, width), jnp.bfloat16),
            pltpu.VMEM((stored, width, width), jnp.bfloat16),
            pltpu.VMEM((batches, shots, rows), jnp.float32),
            pltpu.VMEM((owned, EARLY * CHUNK, width), jnp.bfloat16),
            pltpu.VMEM((EARLY, stored, 2 * CHUNK, width // 2), jnp.bfloat16),
            pltpu.VMEM((owned, 2 * CHUNK, width), jnp.bfloat16),
            pltpu.VMEM((stored, 2 * CHUNK, width // 2), jnp.bfloat16),
            pltpu.VMEM((RING, peers, 2 * CHUNK, width // 2), jnp.bfloat16),
            pltpu.VMEM((chunks, peers + 1, 2 * CHUNK, width // 2), jnp.bfloat16),
            pltpu.VMEM((chunks, 2 * CHUNK, rows // 2), jnp.bfloat16),
            pltpu.VMEM((chunks, 2 * CHUNK, rows // 2), jnp.bfloat16),
            pltpu.VMEM((shots, rows), jnp.float32),
            pltpu.VMEM((8, 128), jnp.int32),
            pltpu.SMEM((8, 128), jnp.int32),
            pltpu.SemaphoreType.DMA((LOADS,)),
            pltpu.SemaphoreType.DMA,
            pltpu.SemaphoreType.DMA((chunks,)),
            pltpu.SemaphoreType.DMA((chunks,)),
            pltpu.SemaphoreType.DMA((chunks, PIECES)),
            pltpu.SemaphoreType.DMA((chunks, PIECES)),
        ],
        compiler_params=pltpu.CompilerParams(
            collective_id=0, has_side_effects=True, vmem_limit_bytes=50 * 1024 * 1024
        ),
        name="sweep",
    )(row_block[0].T, col_block[0], operators[0], sources[0])
    return result[None]


def solution(mesh):
    placed = (
        P("layer", "trace", None, None),
        P("layer", None, "trace", None),
        P("layer", None, None),
        P("layer", "trace", None),
    )
    return jax.shard_map(
        body, mesh=mesh, in_specs=placed, out_specs=P("layer", None, "trace", None), check_vma=False
    )
```
